32 devices in a mesh: row: 16 (over z, y, core), col: 2 (over x).
Axes of the slice: x: 2, y: 2, z: 4, core: 2. Of those that a mesh axis runs over, the one named last changes fastest.
Arguments:
- half_slab: bfloat16 [11264, 4608], P(('row', 'col')), may hold values from -6 to 6
- coef: bfloat16 [4608, 4096], P('row', 'col'), may hold values from -0.01171875 to 0.01171875
- virt_energy: float32 [4096], replicated, may hold values from 0.1 to 4
- occ_energy: float32 [1], replicated, may hold values from -1 to -0.4
- frequency: float32 [3], replicated, may hold values from 0.05 to 3
Outputs:
- polar: float32 [3, 11264, 11264], P(None, 'row', 'col')
The draws below stay inside these ranges and needn't reach their ends.
All inputs are finite; a program needn't handle non-finite values.
Results may differ from the reference program's by a relative error of at most 0.0035.
Values may be sent and summed in bfloat16 or wider, within the bound.
No kernel may reach another device: no remote copies, remote signals or barrier semaphores. Data moves between devices by JAX's collectives and lax.ppermute only.
A program may use at most 320 MiB of HBM per device.

```python
import math
import jax
import jax.numpy as jnp
from jax import lax

AUX = 11264
NAO = 4608
NVIRT = 4096
NFREQ = 3


def steps_of(key, dims, cuts, least, largest):
    loudness = 1.0
    for dim, parts in cuts:
        steps = jax.random.uniform(jax.random.fold_in(jax.random.fold_in(key, 6), dim), (parts,), jnp.float32, least / len(cuts), largest / len(cuts))
        loudness = loudness * jnp.repeat(jnp.exp(steps), dims[dim] // parts).reshape((-1,) + (1,) * (len(dims) - 1 - dim))
    return loudness


def scatter_about(rng, shape, deviation, limit, shards=(), dtype=jnp.bfloat16):
    array = deviation * jax.random.normal(rng, shape, jnp.float32)
    if shards:
        array = array * steps_of(rng, shape, shards, -0.22, 0.18)
    return jnp.clip(array, -limit, limit).astype(dtype)


def setup_inputs(seed: int = 0) -> dict:
    streams_of = jax.random.split(jax.random.key(seed), 6)
    half_slab = scatter_about(streams_of[0], (AUX, NAO), 1.0, 6.0, ((0, 32),))
    coef = scatter_about(streams_of[1], (NAO, NVIRT), (NAO * 64) ** -0.5, 0.01171875, ((0, 16), (1, 2)))
    virt_energy = jnp.clip(jnp.exp(jax.random.uniform(streams_of[2], (NVIRT,), jnp.float32, math.log(0.1), math.log(4.0))), 0.1, 4.0)
    occ_energy = jnp.clip(jax.random.uniform(streams_of[3], (1,), jnp.float32, -1.0, -0.4), -1.0, -0.4)
    frequency = jnp.clip(jnp.exp(jax.random.uniform(streams_of[4], (NFREQ,), jnp.float32, math.log(0.05), math.log(3.0))), 0.05, 3.0)
    return {"half_slab": half_slab, "coef": coef, "virt_energy": virt_energy, "occ_energy": occ_energy, "frequency": frequency}


def reference(half_slab, coef, virt_energy, occ_energy, frequency):
    transformed = jnp.dot(half_slab, coef, preferred_element_type=jnp.float32).astype(jnp.bfloat16)
    energy_gap = virt_energy - occ_energy[0]
    results = []
    for index in range(NFREQ):
        weights = 2.0 * energy_gap / (energy_gap * energy_gap + frequency[index] * frequency[index])
        scaled = (transformed.astype(jnp.float32) * weights[None, :]).astype(jnp.bfloat16)
        results.append(lax.dot_general(scaled, transformed, (((1,), (1,)), ((), ())), preferred_element_type=jnp.float32))
    return jnp.stack(results, 0)
```

```python
import functools

import jax
import jax.numpy as jnp
from jax import lax
from jax.experimental import pallas as pl
from jax.experimental.pallas import tpu as pltpu
from jax.sharding import PartitionSpec as P

AXES = ("row", "col")
BF16, F32 = jnp.bfloat16, jnp.float32
SLAB_PARTS = 5
PARTS = 2


def all_weights(virt_energy, occ_energy, frequency):
    gap = virt_energy - occ_energy[0]
    return 2.0 * gap[None] / (gap[None] * gap[None] + frequency[:, None] * frequency[:, None])


def gathered(half_slab, coef, virt_energy, occ_energy, frequency):
    slab_rows = lax.all_gather(half_slab, "col", axis=0, tiled=True)
    coef_all = lax.all_gather(coef, "row", axis=0, tiled=True)
    block = jnp.dot(slab_rows, coef_all, preferred_element_type=F32).astype(BF16)
    row_panel = lax.all_gather(block, "col", axis=1, tiled=True)
    column_all = lax.all_gather(block, "row", axis=0, tiled=True)
    partner = lax.all_to_all(column_all, "col", split_axis=0, concat_axis=1, tiled=True)
    weights = all_weights(virt_energy, occ_energy, frequency)
    scaled = (row_panel.astype(F32)[None] * weights[:, None, :]).astype(BF16)
    return lax.dot_general(scaled, partner, (((2,), (1,)), ((), ())), preferred_element_type=F32)


def block_kernel(place, scaled, *refs, first):
    pieces, out = refs[:4], refs[-1]
    width = pieces[0].shape[1]
    total = None
    for i, piece in enumerate(pieces):
        term = lax.dot_general(
            scaled[0, :, i * width : (i + 1) * width],
            piece[...],
            (((1,), (1,)), ((), ())),
            preferred_element_type=F32,
        )
        total = term if total is None else total + term
    out[0] = total if first else total + refs[4][0]


def add_block(out, shape, place, scaled, pieces, first):
    freqs, rows, depth = scaled.shape
    cols, width = pieces[0].shape
    tile = rows // 2
    block = pl.BlockSpec((1, tile, cols), lambda f, i, p: (f, i, p[0]))
    in_specs = [pl.BlockSpec((1, tile, depth), lambda f, i, p: (f, i, 0))]
    in_specs += [pl.BlockSpec((cols, width), lambda f, i, p: (0, 0))] * 4
    operands, aliases = [place.reshape(1).astype(jnp.int32), scaled, *pieces], {}
    if out is not None:
        in_specs.append(pl.BlockSpec(memory_space=pl.ANY) if first else block)
        operands.append(out)
        aliases = {6: 0}
    return pl.pallas_call(
        functools.partial(block_kernel, first=first),
        out_shape=jax.ShapeDtypeStruct(shape, F32),
        grid_spec=pltpu.PrefetchScalarGridSpec(
            num_scalar_prefetch=1, grid=(freqs, 2), in_specs=in_specs, out_specs=block
        ),
        input_output_aliases=aliases,
        compiler_params=pltpu.CompilerParams(vmem_limit_bytes=56 * 2**20),
        cost_estimate=pl.CostEstimate(
            flops=2 * freqs * rows * cols * depth,
            bytes_accessed=4 * (2 - first) * freqs * rows * cols + 2 * depth * (freqs * rows + cols),
            transcendentals=0,
        ),
    )(*operands)


def line_plan(half_slab, coef, virt_energy, occ_energy, frequency):
    row, x = lax.axis_index("row"), lax.axis_index("col")
    z, y, k = row // 4, (row // 2) % 2, row % 2
    u = jnp.where(x == 0, z, 3 - z)

    def device(z, y, k, x):
        return ((z * 2 + y) * 2 + k) * 2 + x

    def move(array, target):
        pairs = []
        for dz in range(4):
            for dy in range(2):
                for dk in range(2):
                    for dx in range(2):
                        to = target(dz, dy, dk, dx)
                        if to is not None:
                            pairs.append((device(dz, dy, dk, dx), device(*to)))
        return lax.ppermute(array, AXES, pairs)

    def over_x(a):
        return move(a, lambda z, y, k, x: (z, y, k, 1 - x))

    def over_y(a):
        return move(a, lambda z, y, k, x: (z, 1 - y, k, x))

    def over_k(a):
        return move(a, lambda z, y, k, x: (z, y, 1 - k, x))

    def z_up(a, step):
        return move(a, lambda z, y, k, x: (z + 1, y, k, x) if step - 1 <= z < 3 else None)

    def z_down(a, step):
        return move(a, lambda z, y, k, x: (z - 1, y, k, x) if 0 < z <= 4 - step else None)

    def u_to(a, steps):
        def target(z, y, k, x):
            u = z if x == 0 else 3 - z
            if u not in steps:
                return None
            v = steps[u]
            return (v if x == 0 else 3 - v), y, k, x

        return move(a, target)

    slab_rows, nao = half_slab.shape
    chip_rows = 4 * slab_rows
    rows = chip_rows // 2
    coef_rows, virt_x = coef.shape
    both = virt_x // PARTS
    width = both // 2
    weights = all_weights(virt_energy, occ_energy, frequency)
    freqs = weights.shape[0]
    shape = (freqs, rows, 4 * chip_rows)

    env = {}

    def step(**results):
        env.update(results)
        names = list(env)
        env.update(zip(names, lax.optimization_barrier([env[n] for n in names])))

    def slot(c, n):
        up = [None] + [env.get(f"up{c}{i}") for i in (1, 2, 3)]
        down = [None] + [env.get(f"down{c}{i}") for i in (1, 2, 3)]
        if n == 0:
            return env[f"coef{c}"]
        if n == 1:
            return jnp.where(z == 0, down[1], up[1])
        if n == 2:
            return jnp.where(z == 0, down[2], jnp.where(z == 3, up[2], down[1]))
        return jnp.where(z == 0, down[3], jnp.where(z == 1, down[2], jnp.where(z == 2, up[2], up[3])))

    planes = (
        z,
        jnp.where(z == 0, 1, z - 1),
        jnp.where(z == 0, 2, jnp.where(z == 3, 1, z + 1)),
        jnp.where(z <= 1, 3, 0),
    )

    def line(c, i):
        before = (env[f"coef{c}"],) * 2 if i == 1 else (env[f"up{c}{i - 1}"], env[f"down{c}{i - 1}"])
        return {f"up{c}{i}": z_up(before[0], i), f"down{c}{i}": z_down(before[1], i)}

    def cross(c, n):
        piece = slot(c, n)
        return {f"slot{c}{n}": piece, f"cross{c}{n}": over_y(piece)}

    def cores(c):
        mine = jnp.zeros((8, coef_rows, both), BF16)
        for n in range(4):
            mine = lax.dynamic_update_slice(mine, env.pop(f"slot{c}{n}")[None], (planes[n] * 2 + y, 0, 0))
            mine = lax.dynamic_update_slice(mine, env.pop(f"cross{c}{n}")[None], (planes[n] * 2 + 1 - y, 0, 0))
        theirs = over_k(lax.dynamic_slice(mine, (0, 0, (1 - k) * width), (8, coef_rows, width)))
        return {f"keep{c}": lax.dynamic_slice(mine, (0, 0, k * width), (8, coef_rows, width)), f"theirs{c}": theirs}

    def transformed(c):
        keep, theirs = env.pop(f"keep{c}"), env.pop(f"theirs{c}")
        whole = jnp.where(k == 0, jnp.stack([keep, theirs], 1), jnp.stack([theirs, keep], 1)).reshape(nao, width)
        return {f"own{c}0": jnp.dot(env["slab"], whole, preferred_element_type=F32).astype(BF16)}

    def chip_slab():
        slab = jnp.zeros((4, slab_rows, nao), BF16)
        for name, at in (
            ("slab_o", k * 2 + x),
            ("slab_k", (1 - k) * 2 + x),
            ("slab_x", k * 2 + 1 - x),
            ("slab_kx", (1 - k) * 2 + 1 - x),
        ):
            slab = lax.dynamic_update_slice(slab, env.pop(name)[None], (at, 0, 0))
        return {"slab": slab.reshape(chip_rows, nao)}

    def panel(c):
        parts = []
        for p, v in ((0, x), (1, 1 - x)):
            for held, core in ((env[f"own{c}{p}"], k), (env.pop(f"kown{c}{p}"), 1 - k)):
                of_rows = lax.dynamic_slice(held, (k * rows, 0), (rows, width))
                at = v * virt_x + c * both + core * width
                scale = lax.dynamic_slice(weights, (0, at), (freqs, width))
                parts.append((of_rows.astype(F32)[None] * scale[:, None]).astype(BF16))
        return {f"scaled{c}": jnp.concatenate(parts, 2)}

    items = [(c, near, p) for c in range(PARTS) for near in (1, 0) for p in (0, 1)]
    count = len(items)

    def item(t):
        c, near, p = items[t]
        return env[f"own{c}{p}"] if near else env[f"far{c}{p}"]

    def exchange(c, p):
        return {f"far{c}{p}": u_to(env[f"own{c}{p}"], {0: 1, 1: 0})}

    def along(t):
        if t == 0:
            return {"got0": u_to(item(0), {1: 2})}
        if t == count:
            return {f"got{t}": u_to(env[f"got{t - 1}"], {2: 3})}
        return {f"got{t}": u_to(jnp.where(u == 1, item(t), env[f"got{t - 1}"]), {1: 2, 2: 3})}

    def take(t):
        held = jnp.where(u <= 1, item(t), jnp.where(u == 2, env[f"got{t}"], env[f"got{t + 1}"]))
        return {f"a{t}": held, f"b{t}": over_y(held), f"ka{t}": over_k(held)}

    def take_k(t):
        return {f"kb{t}": over_k(env[f"b{t}"])}

    def block(t, crossed):
        c, near, _ = items[t]
        plane = jnp.where(u == 0, 1 - near, near)
        plane = jnp.where(x == 0, plane, 1 - plane)
        place = plane * 2 + (1 - y if crossed else y)
        s = "b" if crossed else "a"
        pieces = [env.pop(f"{h}{s}{i}") for i in (t, t + 1) for h in ("", "k")]
        env["out"] = add_block(env.get("out"), shape, place, env[f"scaled{c}"], pieces, c == 0)

    for c in range(PARTS):
        env[f"coef{c}"] = coef[:, c * both : (c + 1) * both]
    env["slab_o"] = half_slab
    step()
    cuts = [slab_rows * i // SLAB_PARTS // 16 * 16 for i in range(SLAB_PARTS)] + [slab_rows]

    def slab_part(i):
        return {f"slab_x{i}": over_x(env["slab_o"][cuts[i] : cuts[i + 1]])}

    step(**line(0, 1), **cross(0, 0), **slab_part(0), slab_k=over_k(env["slab_o"]))
    step(**line(0, 2), **cross(0, 1), **slab_part(1))
    step(**line(0, 3), **cross(0, 2), **slab_part(2))
    step(**line(1, 1), **cross(0, 3), **slab_part(3))
    step(**line(1, 2), **cross(1, 0), **cores(0), **slab_part(4))
    env["slab_x"] = jnp.concatenate([env.pop(f"slab_x{i}") for i in range(SLAB_PARTS)], 0)
    step(**line(1, 3), **cross(1, 1), slab_kx=over_k(env["slab_x"]))
    env.update(chip_slab())
    step(**transformed(0))
    step(**cross(1, 2), own01=over_x(env["own00"]), kown00=over_k(env["own00"]), **exchange(0, 0), **along(0))
    step(**cross(1, 3), kown01=over_k(env["own01"]), **exchange(0, 1), **along(1))
    step(**along(2), **take(0), **panel(0), **cores(1))
    r = along(3) | take(1) | take_k(0)
    env.update(transformed(1))
    step(**r)
    for t in range(2, count + 1):
        r = take(t) if t < count else {}
        r |= take_k(t - 1)
        if t + 2 <= count:
            r |= along(t + 2)
        if t == 2:
            r |= dict(own11=over_x(env["own10"]), kown10=over_k(env["own10"])) | exchange(1, 0)
        if t == 3:
            r |= dict(kown11=over_k(env["own11"])) | exchange(1, 1)
        if t == 4:
            r |= panel(1)
        if t % 2 == 0:
            block(t - 2, False)
        elif t > 2:
            block(t - 3, True)
        step(**r)
    block(count - 2, True)
    return env["out"]


def solution(mesh):
    in_specs = (P(("row", "col"), None), P("row", "col"), P(), P(), P())
    out_specs = P(None, "row", "col")
    lines = mesh.shape["row"] == 16 and mesh.shape["col"] == 2
    body = line_plan if lines else gathered
    return jax.shard_map(body, mesh=mesh, in_specs=in_specs, out_specs=out_specs, check_vma=False)
```

```python
import functools

import jax
import jax.numpy as jnp
from jax import lax
from jax.experimental import pallas as pl
from jax.experimental.pallas import tpu as pltpu
from jax.sharding import PartitionSpec as P

AXES = ("row", "col")
BF16, F32 = jnp.bfloat16, jnp.float32
SLAB_PARTS = 3
PARTS = 2


def all_weights(virt_energy, occ_energy, frequency):
    gap = virt_energy - occ_energy[0]
    return 2.0 * gap[None] / (gap[None] * gap[None] + frequency[:, None] * frequency[:, None])


def gathered(half_slab, coef, virt_energy, occ_energy, frequency):
    slab_rows = lax.all_gather(half_slab, "col", axis=0, tiled=True)
    coef_all = lax.all_gather(coef, "row", axis=0, tiled=True)
    block = jnp.dot(slab_rows, coef_all, preferred_element_type=F32).astype(BF16)
    row_panel = lax.all_gather(block, "col", axis=1, tiled=True)
    column_all = lax.all_gather(block, "row", axis=0, tiled=True)
    partner = lax.all_to_all(column_all, "col", split_axis=0, concat_axis=1, tiled=True)
    weights = all_weights(virt_energy, occ_energy, frequency)
    scaled = (row_panel.astype(F32)[None] * weights[:, None, :]).astype(BF16)
    return lax.dot_general(scaled, partner, (((2,), (1,)), ((), ())), preferred_element_type=F32)


def transform_kernel(at, *refs, counts, n_coef):
    n_slab = sum(counts)
    slabs, coefs = refs[:n_slab], refs[n_slab : n_slab + n_coef]
    out, slab_v, coef_v, sems = refs[n_slab + n_coef :]
    rows, width = coefs[0].shape[0], coef_v.shape[1]
    copies = []
    for i, piece in enumerate(coefs):
        first = pl.multiple_of(at[len(counts) + i], 16)
        column = pl.multiple_of(at[len(counts) + n_coef + i], 128)
        copies.append(
            pltpu.make_async_copy(
                piece.at[:, pl.ds(column, width)], coef_v.at[pl.ds(first, rows)], sems.at[n_slab + i]
            )
        )
    groups, used = [], 0
    for count in counts:
        group, begin = [], 0
        for piece in slabs[used : used + count]:
            held = slab_v.at[len(groups), begin : begin + piece.shape[0]]
            group.append(pltpu.make_async_copy(piece, held, sems.at[used + len(group)]))
            begin += piece.shape[0]
        used += count
        groups.append(group)
    for copy in copies + [c for group in groups for c in group]:
        copy.start()
    for copy in copies:
        copy.wait()
    for i, group in enumerate(groups):
        for copy in group:
            copy.wait()
        first = pl.multiple_of(at[i], 16)
        value = jnp.dot(slab_v[i], coef_v[...], preferred_element_type=F32)
        out[pl.ds(first, slab_v.shape[1]), :] = value.astype(out.dtype)


def transform(groups, group_rows, coefs, coef_rows, columns, width):
    slabs = [piece for group in groups for piece in group]
    rows = sum(piece.shape[0] for piece in groups[0])
    depth, nao = len(coefs) * coefs[0].shape[0], slabs[0].shape[1]
    at = jnp.stack([jnp.asarray(v, jnp.int32) for v in (*group_rows, *coef_rows, *columns)])
    total = len(groups) * rows
    return pl.pallas_call(
        functools.partial(transform_kernel, counts=[len(g) for g in groups], n_coef=len(coefs)),
        out_shape=jax.ShapeDtypeStruct((total, width), BF16),
        grid_spec=pltpu.PrefetchScalarGridSpec(
            num_scalar_prefetch=1,
            grid=(1,),
            in_specs=[pl.BlockSpec(memory_space=pl.ANY)] * (len(slabs) + len(coefs)),
            out_specs=pl.BlockSpec((total, width), lambda i, a: (0, 0)),
            scratch_shapes=[
                pltpu.VMEM((len(groups), rows, nao), BF16),
                pltpu.VMEM((depth, width), BF16),
                pltpu.SemaphoreType.DMA((len(slabs) + len(coefs),)),
            ],
        ),
        compiler_params=pltpu.CompilerParams(vmem_limit_bytes=56 * 2**20),
        cost_estimate=pl.CostEstimate(
            flops=2 * total * nao * width, bytes_accessed=2 * (total * nao + nao * width), transcendentals=0
        ),
    )(at, *slabs, *coefs)


def block_kernel(place, scaled, *refs, n_pieces, first):
    pieces, out = refs[:n_pieces], refs[-1]
    width = pieces[0].shape[1]
    total = None
    for i, piece in enumerate(pieces):
        term = lax.dot_general(
            scaled[0, :, i * width : (i + 1) * width],
            piece[...],
            (((1,), (1,)), ((), ())),
            preferred_element_type=F32,
        )
        total = term if total is None else total + term
    out[0] = total if first else total + refs[n_pieces][0]


def add_block(out, shape, place, scaled, pieces, part, first):
    freqs, rows, _ = scaled.shape
    cols, width = pieces[0].shape
    depth = width * len(pieces)
    tile = rows // 2
    block = pl.BlockSpec((1, tile, cols), lambda f, i, p: (f, i, p[0]))
    in_specs = [pl.BlockSpec((1, tile, depth), lambda f, i, p: (f, i, part))]
    in_specs += [pl.BlockSpec((cols, width), lambda f, i, p: (0, 0))] * len(pieces)
    operands, aliases = [place.reshape(1).astype(jnp.int32), scaled, *pieces], {}
    if out is not None:
        in_specs.append(pl.BlockSpec(memory_space=pl.ANY) if first else block)
        aliases = {len(operands): 0}
        operands.append(out)
    return pl.pallas_call(
        functools.partial(block_kernel, n_pieces=len(pieces), first=first),
        out_shape=jax.ShapeDtypeStruct(shape, F32),
        grid_spec=pltpu.PrefetchScalarGridSpec(
            num_scalar_prefetch=1, grid=(freqs, 2), in_specs=in_specs, out_specs=block
        ),
        input_output_aliases=aliases,
        compiler_params=pltpu.CompilerParams(vmem_limit_bytes=56 * 2**20),
        cost_estimate=pl.CostEstimate(
            flops=2 * freqs * rows * cols * depth,
            bytes_accessed=4 * (2 - first) * freqs * rows * cols + 2 * depth * (freqs * rows + cols),
            transcendentals=0,
        ),
    )(*operands)


def line_plan(half_slab, coef, virt_energy, occ_energy, frequency):
    row, x = lax.axis_index("row"), lax.axis_index("col")
    z, y, k = row // 4, (row // 2) % 2, row % 2
    u = jnp.where(x == 0, z, 3 - z)

    def device(z, y, k, x):
        return ((z * 2 + y) * 2 + k) * 2 + x

    def move(array, target):
        pairs = []
        for dz in range(4):
            for dy in range(2):
                for dk in range(2):
                    for dx in range(2):
                        to = target(dz, dy, dk, dx)
                        if to is not None:
                            pairs.append((device(dz, dy, dk, dx), device(*to)))
        return lax.ppermute(array, AXES, pairs)

    def over_x(a):
        return move(a, lambda z, y, k, x: (z, y, k, 1 - x))

    def over_y(a):
        return move(a, lambda z, y, k, x: (z, 1 - y, k, x))

    def over_k(a):
        return move(a, lambda z, y, k, x: (z, y, 1 - k, x))

    def z_up(a, step):
        return move(a, lambda z, y, k, x: (z + 1, y, k, x) if step - 1 <= z < 3 else None)

    def z_down(a, step):
        return move(a, lambda z, y, k, x: (z - 1, y, k, x) if 0 < z <= 4 - step else None)

    def u_to(a, steps):
        def target(z, y, k, x):
            u = z if x == 0 else 3 - z
            if u not in steps:
                return None
            v = steps[u]
            return (v if x == 0 else 3 - v), y, k, x

        return move(a, target)

    slab_rows = half_slab.shape[0]
    chip_rows = 4 * slab_rows
    rows = chip_rows // 2
    coef_rows, virt_x = coef.shape
    both = virt_x // PARTS
    width = both // 2
    weights = all_weights(virt_energy, occ_energy, frequency)
    freqs = weights.shape[0]
    shape = (freqs, rows, 4 * chip_rows)

    env = {}

    def step(**results):
        env.update(results)
        names = list(env)
        env.update(zip(names, lax.optimization_barrier([env[n] for n in names])))

    def slot(n):
        up = [None] + [env.get(f"up{i}") for i in (1, 2, 3)]
        down = [None] + [env.get(f"down{i}") for i in (1, 2, 3)]
        if n == 0:
            return env["coef"]
        if n == 1:
            return jnp.where(z == 0, down[1], up[1])
        if n == 2:
            return jnp.where(z == 0, down[2], jnp.where(z == 3, up[2], down[1]))
        return jnp.where(z == 0, down[3], jnp.where(z == 1, down[2], jnp.where(z == 2, up[2], up[3])))

    planes = (
        z,
        jnp.where(z == 0, 1, z - 1),
        jnp.where(z == 0, 2, jnp.where(z == 3, 1, z + 1)),
        jnp.where(z <= 1, 3, 0),
    )

    def line(i):
        before = (env["coef"],) * 2 if i == 1 else (env[f"up{i - 1}"], env[f"down{i - 1}"])
        return {f"up{i}": z_up(before[0], i), f"down{i}": z_down(before[1], i)}

    def cross(n):
        piece = env[f"slot{n}"] = slot(n)
        return {f"cross{n}": over_y(piece), f"kslot{n}": over_k(piece)}

    def cross_k(n):
        return {f"kcross{n}": over_k(env[f"cross{n}"])}

    cuts = [slab_rows * i // SLAB_PARTS // 16 * 16 for i in range(SLAB_PARTS)] + [slab_rows]

    def slab_part(i):
        return {f"slab_x{i}": over_x(env["slab"][cuts[i] : cuts[i + 1]])}

    def slab_part_k(i):
        return {f"slab_kx{i}": over_k(env[f"slab_x{i}"])}

    def transformed(c):
        groups = [[env["slab"]], [env["slab_k"]]]
        groups += [[env[f"slab_{name}{i}"] for i in range(SLAB_PARTS)] for name in ("x", "kx")]
        group_rows = [
            (core * 2 + side) * slab_rows for side in (x, 1 - x) for core in (k, 1 - k)
        ]
        coefs, coef_at, columns = [], [], []
        for n in range(4):
            for name, at_y in (("slot", y), ("cross", 1 - y)):
                for prefix, core in (("", k), ("k", 1 - k)):
                    whole = env.get(f"{prefix}{name}{n}")
                    coefs.append(env[f"{prefix}{name}{n}_{c}"] if whole is None else whole)
                    columns.append(k * width + (0 if whole is None else c * both))
                    coef_at.append(((planes[n] * 2 + at_y) * 2 + core) * coef_rows)
        return {f"own{c}0": transform(groups, group_rows, coefs, coef_at, columns, width)}

    def panel(c):
        parts = []
        for p, v in ((0, x), (1, 1 - x)):
            for held, core in ((env[f"own{c}{p}"], k), (env.pop(f"kown{c}{p}"), 1 - k)):
                of_rows = lax.dynamic_slice(held, (k * rows, 0), (rows, width))
                at = v * virt_x + c * both + core * width
                scale = lax.dynamic_slice(weights, (0, at), (freqs, width))
                parts.append((of_rows.astype(F32)[None] * scale[:, None]).astype(BF16))
        return {f"scaled{c}": jnp.concatenate(parts, 2)}

    items = [(c, near, p) for c in range(PARTS) for near in (1, 0) for p in (0, 1)]
    count = len(items)

    def item(t):
        c, near, p = items[t]
        return env[f"own{c}{p}"] if near else env[f"far{c}{p}"]

    def exchange(c, p):
        return {f"far{c}{p}": u_to(env[f"own{c}{p}"], {0: 1, 1: 0})}

    def along(t):
        if t == 0:
            return {"got0": u_to(item(0), {1: 2})}
        if t == count:
            return {f"got{t}": u_to(env[f"got{t - 1}"], {2: 3})}
        return {f"got{t}": u_to(jnp.where(u == 1, item(t), env[f"got{t - 1}"]), {1: 2, 2: 3})}

    def take(t):
        held = jnp.where(u <= 1, item(t), jnp.where(u == 2, env[f"got{t}"], env[f"got{t + 1}"]))
        return {f"a{t}": held, f"b{t}": over_y(held), f"ka{t}": over_k(held)}

    def taken(t):
        return {f"kb{t}": over_k(env[f"b{t}"])}

    def block(t, crossed, pieces_of, part, first):
        c, near, _ = items[t]
        plane = jnp.where(u == 0, 1 - near, near)
        plane = jnp.where(x == 0, plane, 1 - plane)
        place = plane * 2 + (1 - y if crossed else y)
        env["out"] = add_block(env.get("out"), shape, place, env[f"scaled{c}"], pieces_of, part, first)

    env["coef"], env["slab"] = coef, half_slab
    step(**line(1), **cross(0), **slab_part(0), slab_k=over_k(env["slab"]))
    step(**line(2), **cross(1), **slab_part(1), **slab_part_k(0), **cross_k(0))
    step(**line(3), **cross(2), **slab_part(2), **slab_part_k(1), **cross_k(1))
    env["slot3"] = slot(3)
    halves = [env["slot3"][:, c * both : (c + 1) * both] for c in range(PARTS)]
    env.update(later=halves[1])
    step(cross3_0=over_y(halves[0]), kslot3=over_k(env["slot3"]), **slab_part_k(2), **cross_k(2))
    env["kcross3_0"] = over_k(env["cross3_0"])
    step(**transformed(0))

    for t in range(count + 2):
        r = along(t) if t <= count else {}
        if t == 0:
            r |= dict(cross3_1=over_y(env.pop("later")))
            r |= dict(own01=over_x(env["own00"]), kown00=over_k(env["own00"])) | exchange(0, 0)
        if t == 1:
            env["kcross3_1"] = over_k(env["cross3_1"])
            r |= dict(kown01=over_k(env["own01"])) | exchange(0, 1)
            r |= transformed(1)
        if t == 2:
            r |= panel(0) | exchange(1, 0)
            r |= dict(own11=over_x(env["own10"]), kown10=over_k(env["own10"]))
        if t == 3:
            r |= dict(kown11=over_k(env["own11"])) | exchange(1, 1)
        if t == 5:
            r |= panel(1)
        if t >= 2:
            r |= take(t - 2)
        if t >= 3:
            r |= taken(t - 3)
        if t >= 3 and t % 2 == 1:
            i = t - 3
            pieces = [env.pop(f"a{i}"), env.pop(f"ka{i}"), r.pop(f"a{i + 1}"), r.pop(f"ka{i + 1}")]
            block(i, False, pieces, 0, i < count // PARTS)
        if t >= 4 and t % 2 == 0:
            i = t - 4
            pieces = [env.pop(f"b{i}"), env.pop(f"kb{i}"), env.pop(f"b{i + 1}"), r.pop(f"kb{i + 1}")]
            block(i, True, pieces, 0, i < count // PARTS)
        if t == count + 1:
            block(count - 2, True, [env.pop(f"b{count - 2}"), r.pop(f"kb{count - 2}")], 0, False)
        step(**r)
    block(count - 2, True, [env[f"b{count - 1}"], taken(count - 1)[f"kb{count - 1}"]], 1, False)
    return env["out"]


def solution(mesh):
    in_specs = (P(("row", "col"), None), P("row", "col"), P(), P(), P())
    out_specs = P(None, "row", "col")
    lines = mesh.shape["row"] == 16 and mesh.shape["col"] == 2
    body = line_plan if lines else gathered
    return jax.shard_map(body, mesh=mesh, in_specs=in_specs, out_specs=out_specs, check_vma=False)
```

```python
import functools

import jax
import jax.numpy as jnp
from jax import lax
from jax.experimental import pallas as pl
from jax.experimental.pallas import tpu as pltpu
from jax.sharding import PartitionSpec as P

AXES = ("row", "col")
BF16, F32 = jnp.bfloat16, jnp.float32
SLAB_PARTS = 3
PARTS = 2


def all_weights(virt_energy, occ_energy, frequency):
    gap = virt_energy - occ_energy[0]
    return 2.0 * gap[None] / (gap[None] * gap[None] + frequency[:, None] * frequency[:, None])


def gathered(half_slab, coef, virt_energy, occ_energy, frequency):
    slab_rows = lax.all_gather(half_slab, "col", axis=0, tiled=True)
    coef_all = lax.all_gather(coef, "row", axis=0, tiled=True)
    block = jnp.dot(slab_rows, coef_all, preferred_element_type=F32).astype(BF16)
    row_panel = lax.all_gather(block, "col", axis=1, tiled=True)
    column_all = lax.all_gather(block, "row", axis=0, tiled=True)
    partner = lax.all_to_all(column_all, "col", split_axis=0, concat_axis=1, tiled=True)
    weights = all_weights(virt_energy, occ_energy, frequency)
    scaled = (row_panel.astype(F32)[None] * weights[:, None, :]).astype(BF16)
    return lax.dot_general(scaled, partner, (((2,), (1,)), ((), ())), preferred_element_type=F32)


def transform_kernel(at, *refs, counts, n_coef):
    n_slab = sum(counts)
    slabs, coefs = refs[:n_slab], refs[n_slab : n_slab + n_coef]
    out, slab_v, coef_v, sems = refs[n_slab + n_coef :]
    rows, width = coefs[0].shape[0], coef_v.shape[1]
    copies = []
    for i, piece in enumerate(coefs):
        first = pl.multiple_of(at[len(counts) + i], 16)
        column = pl.multiple_of(at[len(counts) + n_coef + i], 128)
        copies.append(
            pltpu.make_async_copy(
                piece.at[:, pl.ds(column, width)], coef_v.at[pl.ds(first, rows)], sems.at[n_slab + i]
            )
        )
    groups, used = [], 0
    for count in counts:
        group, begin = [], 0
        for piece in slabs[used : used + count]:
            held = slab_v.at[len(groups), begin : begin + piece.shape[0]]
            group.append(pltpu.make_async_copy(piece, held, sems.at[used + len(group)]))
            begin += piece.shape[0]
        used += count
        groups.append(group)
    for copy in copies + [c for group in groups for c in group]:
        copy.start()
    for copy in copies:
        copy.wait()
    for i, group in enumerate(groups):
        for copy in group:
            copy.wait()
        first = pl.multiple_of(at[i], 16)
        value = jnp.dot(slab_v[i], coef_v[...], preferred_element_type=F32)
        out[pl.ds(first, slab_v.shape[1]), :] = value.astype(out.dtype)


def transform(groups, group_rows, coefs, coef_rows, columns, width):
    slabs = [piece for group in groups for piece in group]
    rows = sum(piece.shape[0] for piece in groups[0])
    depth, nao = len(coefs) * coefs[0].shape[0], slabs[0].shape[1]
    at = jnp.stack([jnp.asarray(v, jnp.int32) for v in (*group_rows, *coef_rows, *columns)])
    total = len(groups) * rows
    return pl.pallas_call(
        functools.partial(transform_kernel, counts=[len(g) for g in groups], n_coef=len(coefs)),
        out_shape=jax.ShapeDtypeStruct((total, width), BF16),
        grid_spec=pltpu.PrefetchScalarGridSpec(
            num_scalar_prefetch=1,
            grid=(1,),
            in_specs=[pl.BlockSpec(memory_space=pl.ANY)] * (len(slabs) + len(coefs)),
            out_specs=pl.BlockSpec((total, width), lambda i, a: (0, 0)),
            scratch_shapes=[
                pltpu.VMEM((len(groups), rows, nao), BF16),
                pltpu.VMEM((depth, width), BF16),
                pltpu.SemaphoreType.DMA((len(slabs) + len(coefs),)),
            ],
        ),
        compiler_params=pltpu.CompilerParams(vmem_limit_bytes=56 * 2**20),
        cost_estimate=pl.CostEstimate(
            flops=2 * total * nao * width, bytes_accessed=2 * (total * nao + nao * width), transcendentals=0
        ),
    )(at, *slabs, *coefs)


def block_kernel(place, scaled, *refs, n_pieces, first):
    pieces, out = refs[:n_pieces], refs[-1]
    width = pieces[0].shape[1]
    total = None
    for i, piece in enumerate(pieces):
        term = lax.dot_general(
            scaled[0, :, i * width : (i + 1) * width],
            piece[...],
            (((1,), (1,)), ((), ())),
            preferred_element_type=F32,
        )
        total = term if total is None else total + term
    out[0] = total if first else total + refs[n_pieces][0]


def add_block(out, shape, place, scaled, pieces, part, first):
    freqs, rows, _ = scaled.shape
    cols, width = pieces[0].shape
    depth = width * len(pieces)
    tile = rows // 2
    block = pl.BlockSpec((1, tile, cols), lambda f, i, p: (f, i, p[0]))
    in_specs = [pl.BlockSpec((1, tile, depth), lambda f, i, p: (f, i, part))]
    in_specs += [pl.BlockSpec((cols, width), lambda f, i, p: (0, 0))] * len(pieces)
    operands, aliases = [place.reshape(1).astype(jnp.int32), scaled, *pieces], {}
    if out is not None:
        in_specs.append(pl.BlockSpec(memory_space=pl.ANY) if first else block)
        aliases = {len(operands): 0}
        operands.append(out)
    return pl.pallas_call(
        functools.partial(block_kernel, n_pieces=len(pieces), first=first),
        out_shape=jax.ShapeDtypeStruct(shape, F32),
        grid_spec=pltpu.PrefetchScalarGridSpec(
            num_scalar_prefetch=1, grid=(freqs, 2), in_specs=in_specs, out_specs=block
        ),
        input_output_aliases=aliases,
        compiler_params=pltpu.CompilerParams(vmem_limit_bytes=56 * 2**20),
        cost_estimate=pl.CostEstimate(
            flops=2 * freqs * rows * cols * depth,
            bytes_accessed=4 * (2 - first) * freqs * rows * cols + 2 * depth * (freqs * rows + cols),
            transcendentals=0,
        ),
    )(*operands)


def line_plan(half_slab, coef, virt_energy, occ_energy, frequency):
    row, x = lax.axis_index("row"), lax.axis_index("col")
    z, y, k = row // 4, (row // 2) % 2, row % 2
    u = jnp.where(x == 0, z, 3 - z)

    def device(z, y, k, x):
        return ((z * 2 + y) * 2 + k) * 2 + x

    def move(array, target):
        pairs = []
        for dz in range(4):
            for dy in range(2):
                for dk in range(2):
                    for dx in range(2):
                        to = target(dz, dy, dk, dx)
                        if to is not None:
                            pairs.append((device(dz, dy, dk, dx), device(*to)))
        return lax.ppermute(array, AXES, pairs)

    def over_x(a):
        return move(a, lambda z, y, k, x: (z, y, k, 1 - x))

    def over_y(a):
        return move(a, lambda z, y, k, x: (z, 1 - y, k, x))

    def over_k(a):
        return move(a, lambda z, y, k, x: (z, y, 1 - k, x))

    def z_up(a, step):
        return move(a, lambda z, y, k, x: (z + 1, y, k, x) if step - 1 <= z < 3 else None)

    def z_down(a, step):
        return move(a, lambda z, y, k, x: (z - 1, y, k, x) if 0 < z <= 4 - step else None)

    slab_rows = half_slab.shape[0]
    chip_rows = 4 * slab_rows
    rows = chip_rows // 2
    coef_rows, virt_x = coef.shape
    both = virt_x // PARTS
    width = both // 2
    weights = all_weights(virt_energy, occ_energy, frequency)
    freqs = weights.shape[0]
    shape = (freqs, rows, 4 * chip_rows)

    env = {}

    def step(**results):
        env.update(results)
        names = list(env)
        env.update(zip(names, lax.optimization_barrier([env[n] for n in names])))

    def slot(n):
        up = [None] + [env.get(f"up{i}") for i in (1, 2, 3)]
        down = [None] + [env.get(f"down{i}") for i in (1, 2, 3)]
        if n == 0:
            return env["coef"]
        if n == 1:
            return jnp.where(z == 0, down[1], up[1])
        if n == 2:
            return jnp.where(z == 0, down[2], jnp.where(z == 3, up[2], down[1]))
        return jnp.where(z == 0, down[3], jnp.where(z == 1, down[2], jnp.where(z == 2, up[2], up[3])))

    planes = (
        z,
        jnp.where(z == 0, 1, z - 1),
        jnp.where(z == 0, 2, jnp.where(z == 3, 1, z + 1)),
        jnp.where(z <= 1, 3, 0),
    )

    def line(i):
        before = (env["coef"],) * 2 if i == 1 else (env[f"up{i - 1}"], env[f"down{i - 1}"])
        return {f"up{i}": z_up(before[0], i), f"down{i}": z_down(before[1], i)}

    def cross(n):
        piece = env[f"slot{n}"] = slot(n)
        return {f"cross{n}": over_y(piece), f"kslot{n}": over_k(piece)}

    def cross_k(n):
        return {f"kcross{n}": over_k(env[f"cross{n}"])}

    cuts = [slab_rows * i // SLAB_PARTS // 16 * 16 for i in range(SLAB_PARTS)] + [slab_rows]

    def slab_part(i):
        return {f"slab_x{i}": over_x(env["slab"][:cuts[1]] if i == 0 else env.pop(f"slab{i}"))}

    def slab_part_k(i):
        return {f"slab_kx{i}": over_k(env[f"slab_x{i}"])}

    def transformed(c):
        groups = [[env["slab"]], [env["slab_k"]]]
        groups += [[env[f"slab_{name}{i}"] for i in range(SLAB_PARTS)] for name in ("x", "kx")]
        group_rows = [
            (core * 2 + side) * slab_rows for side in (x, 1 - x) for core in (k, 1 - k)
        ]
        coefs, coef_at, columns = [], [], []
        for n in range(4):
            for name, at_y in (("slot", y), ("cross", 1 - y)):
                for prefix, core in (("", k), ("k", 1 - k)):
                    whole = env.get(f"{prefix}{name}{n}")
                    coefs.append(env[f"{prefix}{name}{n}_{c}"] if whole is None else whole)
                    columns.append(k * width + (0 if whole is None else c * both))
                    coef_at.append(((planes[n] * 2 + at_y) * 2 + core) * coef_rows)
        return {f"own{c}": transform(groups, group_rows, coefs, coef_at, columns, width)}

    def panel(c):
        parts = []
        for p, v in ((0, x), (1, 1 - x)):
            name = ("own", "own_x")[p] + str(c)
            for held, core in ((env[name], k), (env.pop("k" + name), 1 - k)):
                of_rows = lax.dynamic_slice(held, (k * rows, 0), (rows, width))
                at = v * virt_x + c * both + core * width
                scale = lax.dynamic_slice(weights, (0, at), (freqs, width))
                parts.append((of_rows.astype(F32)[None] * scale[:, None]).astype(BF16))
        return {f"scaled{c}": jnp.concatenate(parts, 2)}

    home = u <= 1
    inner = (z == 1) | (z == 2)

    def planes_swap(a, pairs):
        return move(a, lambda z, y, k, x: (pairs[z], y, k, x) if z in pairs else None)

    def to_visitor(a):
        return move(a, lambda z, y, k, x: (z, y, k, 1 - x) if x == z // 2 else None)

    def here(s):
        return env[f"{('own', 'far')[s % 2]}{s // 2}"]

    def inward(s):
        return {f"mid{s}": planes_swap(here(s), {1: 2, 2: 1})}

    def outward(s):
        return {f"out{s}": planes_swap(env[f"mid{s}"], {1: 0, 2: 3})}

    def exchange(c):
        return {f"far{c}": planes_swap(env[f"own{c}"], {0: 1, 1: 0, 2: 3, 3: 2})}

    def own_x(c):
        return {f"own_x{c}": over_x(env[f"own{c}"])}

    def choose(s):
        visiting = jnp.where(inner, env.pop(f"mid{s}"), env.pop(f"out{s}"))
        env[f"o{s}"] = jnp.where(home, here(s), visiting)
        if s % 2:
            return {f"c{s}": over_x(jnp.where(home, visiting, here(s)))}
        return {f"x{s}": to_visitor(visiting)}

    def join(s):
        env[f"c{s}"] = jnp.where(home, env[f"own_x{s // 2}"], env.pop(f"x{s}"))

    def cross_y(name):
        return {f"y{name}": over_y(env[name])}

    def cross_core(*names):
        return {f"k{name}": over_k(env[name]) for name in names}

    def block(s, crossed, new):
        env.update(new)
        near = 1 - s % 2
        plane = jnp.where(u == 0, 1 - near, near)
        plane = jnp.where(x == 0, plane, 1 - plane)
        place = plane * 2 + (1 - y if crossed else y)
        names = [f"{q}{p}{s}" for p in (("yo", "yc") if crossed else ("o", "c")) for q in ("", "k")]
        pieces = [env.pop(n) if crossed or n[0] == "k" else env[n] for n in names]
        env["out"] = add_block(env.get("out"), shape, place, env[f"scaled{s // 2}"], pieces, 0, s < 2)

    env["coef"], env["slab"] = coef, half_slab
    parts = {f"slab{i}": env["slab"][cuts[i] : cuts[i + 1]] for i in range(1, SLAB_PARTS)}
    step(**line(1), **cross(0), **slab_part(0), **parts, slab_k=over_k(env["slab"]))
    step(**line(2), **cross(1), **slab_part(1), **slab_part_k(0), **cross_k(0))
    step(**line(3), **cross(2), **slab_part(2), **slab_part_k(1), **cross_k(1))
    env["slot3"] = slot(3)
    halves = [env["slot3"][:, c * both : (c + 1) * both] for c in range(PARTS)]
    env.update(later=halves[1])
    step(cross3_0=over_y(halves[0]), kslot3=over_k(env["slot3"]), **slab_part_k(2), **cross_k(2))
    env["kcross3_0"] = over_k(env["cross3_0"])
    step(**transformed(0))

    first = inward(0) | exchange(0) | own_x(0) | cross_core("own0")
    env["cross3_1"] = over_y(env.pop("later"))
    env["kcross3_1"] = over_k(env["cross3_1"])
    step(**first, **transformed(1))
    step(**inward(1), **outward(0), **own_x(1), **cross_core("own1", "own_x0"))
    r = choose(0) | cross_y("o0") | cross_core("o0", "own_x1")
    step(**r, **inward(2), **exchange(1), **panel(0))
    join(0)
    r = cross_y("c0") | inward(3) | outward(1) | cross_core("yo0")
    block(0, False, cross_core("c0"))
    step(**r)
    r = choose(1) | cross_y("o1") | outward(2) | cross_core("o1")
    block(0, True, cross_core("yc0"))
    step(**r)
    r = choose(2) | cross_y("c1") | outward(3) | cross_core("o2", "yo1") | panel(1)
    block(1, False, cross_core("c1"))
    step(**r)
    join(2)
    r = cross_y("o2") | cross_y("c2") | choose(3) | cross_core("o3")
    block(1, True, cross_core("yc1"))
    block(2, False, cross_core("c2"))
    step(**r)
    r = cross_y("o3") | cross_y("c3")
    block(3, False, cross_core("c3"))
    block(2, True, cross_core("yo2", "yc2"))
    step(**r)
    block(3, True, cross_core("yo3", "yc3"))
    return env["out"]


def solution(mesh):
    in_specs = (P(("row", "col"), None), P("row", "col"), P(), P(), P())
    out_specs = P(None, "row", "col")
    lines = mesh.shape["row"] == 16 and mesh.shape["col"] == 2
    body = line_plan if lines else gathered
    return jax.shard_map(body, mesh=mesh, in_specs=in_specs, out_specs=out_specs, check_vma=False)
```

```python
import functools

import jax
import jax.numpy as jnp
from jax import lax
from jax.experimental import pallas as pl
from jax.experimental.pallas import tpu as pltpu
from jax.sharding import PartitionSpec as P

AXES = ("row", "col")
BF16, F32 = jnp.bfloat16, jnp.float32
SLAB_PARTS = 3
PARTS = 2


def all_weights(virt_energy, occ_energy, frequency):
    gap = virt_energy - occ_energy[0]
    return 2.0 * gap[None] / (gap[None] * gap[None] + frequency[:, None] * frequency[:, None])


def gathered(half_slab, coef, virt_energy, occ_energy, frequency):
    slab_rows = lax.all_gather(half_slab, "col", axis=0, tiled=True)
    coef_all = lax.all_gather(coef, "row", axis=0, tiled=True)
    block = jnp.dot(slab_rows, coef_all, preferred_element_type=F32).astype(BF16)
    row_panel = lax.all_gather(block, "col", axis=1, tiled=True)
    column_all = lax.all_gather(block, "row", axis=0, tiled=True)
    partner = lax.all_to_all(column_all, "col", split_axis=0, concat_axis=1, tiled=True)
    weights = all_weights(virt_energy, occ_energy, frequency)
    scaled = (row_panel.astype(F32)[None] * weights[:, None, :]).astype(BF16)
    return lax.dot_general(scaled, partner, (((2,), (1,)), ((), ())), preferred_element_type=F32)


def transform_kernel(at, *refs, counts, n_coef):
    n_slab = sum(counts)
    slabs, coefs = refs[:n_slab], refs[n_slab : n_slab + n_coef]
    out, slab_v, coef_v, sems = refs[n_slab + n_coef :]
    rows, width = coefs[0].shape[0], coef_v.shape[1]
    copies = []
    for i, piece in enumerate(coefs):
        first = pl.multiple_of(at[len(counts) + i], 16)
        column = pl.multiple_of(at[len(counts) + n_coef + i], 128)
        copies.append(
            pltpu.make_async_copy(
                piece.at[:, pl.ds(column, width)], coef_v.at[pl.ds(first, rows)], sems.at[n_slab + i]
            )
        )
    groups, used = [], 0
    for count in counts:
        group, begin = [], 0
        for piece in slabs[used : used + count]:
            held = slab_v.at[len(groups), begin : begin + piece.shape[0]]
            group.append(pltpu.make_async_copy(piece, held, sems.at[used + len(group)]))
            begin += piece.shape[0]
        used += count
        groups.append(group)
    for copy in copies + groups[0]:
        copy.start()
    for copy in copies:
        copy.wait()
    for i, group in enumerate(groups):
        for copy in groups[i + 1] if i + 1 < len(groups) else []:
            copy.start()
        for copy in group:
            copy.wait()
        first = pl.multiple_of(at[i], 16)
        value = jnp.dot(slab_v[i], coef_v[...], preferred_element_type=F32)
        out[pl.ds(first, slab_v.shape[1]), :] = value.astype(out.dtype)


def transform(groups, group_rows, coefs, coef_rows, columns, width):
    slabs = [piece for group in groups for piece in group]
    rows = sum(piece.shape[0] for piece in groups[0])
    depth, nao = len(coefs) * coefs[0].shape[0], slabs[0].shape[1]
    at = jnp.stack([jnp.asarray(v, jnp.int32) for v in (*group_rows, *coef_rows, *columns)])
    total = len(groups) * rows
    return pl.pallas_call(
        functools.partial(transform_kernel, counts=[len(g) for g in groups], n_coef=len(coefs)),
        out_shape=jax.ShapeDtypeStruct((total, width), BF16),
        grid_spec=pltpu.PrefetchScalarGridSpec(
            num_scalar_prefetch=1,
            grid=(1,),
            in_specs=[pl.BlockSpec(memory_space=pl.ANY)] * (len(slabs) + len(coefs)),
            out_specs=pl.BlockSpec((total, width), lambda i, a: (0, 0)),
            scratch_shapes=[
                pltpu.VMEM((len(groups), rows, nao), BF16),
                pltpu.VMEM((depth, width), BF16),
                pltpu.SemaphoreType.DMA((len(slabs) + len(coefs),)),
            ],
        ),
        compiler_params=pltpu.CompilerParams(vmem_limit_bytes=56 * 2**20),
        cost_estimate=pl.CostEstimate(
            flops=2 * total * nao * width, bytes_accessed=2 * (total * nao + nao * width), transcendentals=0
        ),
    )(at, *slabs, *coefs)


def block_kernel(place, scaled, *refs, n_pieces, first):
    pieces, out = refs[:n_pieces], refs[-1]
    width = pieces[0].shape[1]
    total = None
    for i, piece in enumerate(pieces):
        term = lax.dot_general(
            scaled[0, :, i * width : (i + 1) * width],
            piece[...],
            (((1,), (1,)), ((), ())),
            preferred_element_type=F32,
        )
        total = term if total is None else total + term
    out[0] = total if first else total + refs[n_pieces][0]


def add_block(out, shape, place, scaled, pieces, part, first, tiles=2):
    freqs, rows, _ = scaled.shape
    cols, width = pieces[0].shape
    depth = width * len(pieces)
    tile = rows // tiles
    block = pl.BlockSpec((1, tile, cols), lambda f, i, p: (f, i, p[0]))
    in_specs = [pl.BlockSpec((1, tile, depth), lambda f, i, p: (f, i, part))]
    in_specs += [pl.BlockSpec((cols, width), lambda f, i, p: (0, 0))] * len(pieces)
    operands, aliases = [place.reshape(1).astype(jnp.int32), scaled, *pieces], {}
    if out is not None:
        in_specs.append(pl.BlockSpec(memory_space=pl.ANY) if first else block)
        aliases = {len(operands): 0}
        operands.append(out)
    return pl.pallas_call(
        functools.partial(block_kernel, n_pieces=len(pieces), first=first),
        out_shape=jax.ShapeDtypeStruct(shape, F32),
        grid_spec=pltpu.PrefetchScalarGridSpec(
            num_scalar_prefetch=1, grid=(freqs, tiles), in_specs=in_specs, out_specs=block
        ),
        input_output_aliases=aliases,
        compiler_params=pltpu.CompilerParams(vmem_limit_bytes=56 * 2**20),
        cost_estimate=pl.CostEstimate(
            flops=2 * freqs * rows * cols * depth,
            bytes_accessed=4 * (2 - first) * freqs * rows * cols + 2 * depth * (freqs * rows + cols),
            transcendentals=0,
        ),
    )(*operands)


def line_plan(half_slab, coef, virt_energy, occ_energy, frequency):
    row, x = lax.axis_index("row"), lax.axis_index("col")
    z, y, k = row // 4, (row // 2) % 2, row % 2
    u = jnp.where(x == 0, z, 3 - z)

    def device(z, y, k, x):
        return ((z * 2 + y) * 2 + k) * 2 + x

    def move(array, target):
        pairs = []
        for dz in range(4):
            for dy in range(2):
                for dk in range(2):
                    for dx in range(2):
                        to = target(dz, dy, dk, dx)
                        if to is not None:
                            pairs.append((device(dz, dy, dk, dx), device(*to)))
        return lax.ppermute(array, AXES, pairs)

    def over_x(a):
        return move(a, lambda z, y, k, x: (z, y, k, 1 - x))

    def over_y(a):
        return move(a, lambda z, y, k, x: (z, 1 - y, k, x))

    def over_k(a):
        return move(a, lambda z, y, k, x: (z, y, 1 - k, x))

    def z_up(a, step):
        return move(a, lambda z, y, k, x: (z + 1, y, k, x) if step - 1 <= z < 3 else None)

    def z_down(a, step):
        return move(a, lambda z, y, k, x: (z - 1, y, k, x) if 0 < z <= 4 - step else None)

    slab_rows = half_slab.shape[0]
    chip_rows = 4 * slab_rows
    rows = chip_rows // 2
    coef_rows, virt_x = coef.shape
    both = virt_x // PARTS
    width = both // 2
    weights = all_weights(virt_energy, occ_energy, frequency)
    freqs = weights.shape[0]
    shape = (freqs, rows, 4 * chip_rows)

    env = {}

    def step(**results):
        env.update(results)
        names = list(env)
        env.update(zip(names, lax.optimization_barrier([env[n] for n in names])))

    def slot(n):
        up = [None] + [env.get(f"up{i}") for i in (1, 2, 3)]
        down = [None] + [env.get(f"down{i}") for i in (1, 2, 3)]
        if n == 0:
            return env["coef"]
        if n == 1:
            return jnp.where(z == 0, down[1], up[1])
        if n == 2:
            return jnp.where(z == 0, down[2], jnp.where(z == 3, up[2], down[1]))
        return jnp.where(z == 0, down[3], jnp.where(z == 1, down[2], jnp.where(z == 2, up[2], up[3])))

    planes = (
        z,
        jnp.where(z == 0, 1, z - 1),
        jnp.where(z == 0, 2, jnp.where(z == 3, 1, z + 1)),
        jnp.where(z <= 1, 3, 0),
    )

    def line(i):
        before = (env["coef"],) * 2 if i == 1 else (env[f"up{i - 1}"], env[f"down{i - 1}"])
        return {f"up{i}": z_up(before[0], i), f"down{i}": z_down(before[1], i)}

    def cross(n):
        piece = env[f"slot{n}"] = slot(n)
        return {f"cross{n}": over_y(piece), f"kslot{n}": over_k(piece)}

    def cross_k(n):
        return {f"kcross{n}": over_k(env[f"cross{n}"])}

    cuts = [slab_rows * i // 11 // 16 * 16 for i in (0, 3, 7)] + [slab_rows]

    def slab_part(i):
        return {f"slab_x{i}": over_x(env["slab"][:cuts[1]] if i == 0 else env.pop(f"slab{i}"))}

    def slab_part_k(i):
        return {f"slab_kx{i}": over_k(env[f"slab_x{i}"])}

    def transformed(c):
        groups = [[env["slab"]], [env["slab_k"]]]
        groups += [[env[f"slab_{name}{i}"] for i in range(SLAB_PARTS)] for name in ("x", "kx")]
        group_rows = [
            (core * 2 + side) * slab_rows for side in (x, 1 - x) for core in (k, 1 - k)
        ]
        coefs, coef_at, columns = [], [], []
        for n in range(4):
            for name, at_y in (("slot", y), ("cross", 1 - y)):
                for prefix, core in (("", k), ("k", 1 - k)):
                    whole = env.get(f"{prefix}{name}{n}")
                    coefs.append(env[f"{prefix}{name}{n}_{c}"] if whole is None else whole)
                    columns.append(k * width + (0 if whole is None else c * both))
                    coef_at.append(((planes[n] * 2 + at_y) * 2 + core) * coef_rows)
        return {f"own{c}": transform(groups, group_rows, coefs, coef_at, columns, width)}

    def panel(c):
        parts = []
        for p, v in ((0, x), (1, 1 - x)):
            name = ("own", "own_x")[p] + str(c)
            for held, core in ((env[name], k), (env.pop("k" + name), 1 - k)):
                of_rows = lax.dynamic_slice(held, (k * rows, 0), (rows, width))
                at = v * virt_x + c * both + core * width
                scale = lax.dynamic_slice(weights, (0, at), (freqs, width))
                parts.append((of_rows.astype(F32)[None] * scale[:, None]).astype(BF16))
        return {f"scaled{c}": jnp.concatenate(parts, 2)}

    home = u <= 1
    inner = (z == 1) | (z == 2)

    def planes_swap(a, pairs):
        return move(a, lambda z, y, k, x: (pairs[z], y, k, x) if z in pairs else None)

    def to_visitor(a):
        return move(a, lambda z, y, k, x: (z, y, k, 1 - x) if x == z // 2 else None)

    def here(s):
        return env[f"{('own', 'far')[s % 2]}{s // 2}"]

    def inward(s):
        return {f"mid{s}": planes_swap(here(s), {1: 2, 2: 1})}

    def outward(s):
        return {f"out{s}": planes_swap(env[f"mid{s}"], {1: 0, 2: 3})}

    def exchange(c):
        return {f"far{c}": planes_swap(env[f"own{c}"], {0: 1, 1: 0, 2: 3, 3: 2})}

    def own_x(c):
        return {f"own_x{c}": over_x(env[f"own{c}"])}

    def choose(s):
        visiting = jnp.where(inner, env.pop(f"mid{s}"), env.pop(f"out{s}"))
        env[f"o{s}"] = jnp.where(home, here(s), visiting)
        if s % 2:
            return {f"c{s}": over_x(jnp.where(home, visiting, here(s)))}
        return {f"x{s}": to_visitor(visiting)}

    def join(s):
        env[f"c{s}"] = jnp.where(home, env[f"own_x{s // 2}"], env.pop(f"x{s}"))

    def cross_y(name):
        return {f"y{name}": over_y(env[name])}

    def cross_core(*names):
        return {f"k{name}": over_k(env[name]) for name in names}

    def block(s, crossed, new, half=None):
        env.update(new)
        near = 1 - s % 2
        plane = jnp.where(u == 0, 1 - near, near)
        plane = jnp.where(x == 0, plane, 1 - plane)
        place = plane * 2 + (1 - y if crossed else y)
        names = [f"{q}{p}{s}" for p in (("yo", "yc") if crossed else ("o", "c")) for q in ("", "k")]
        if half is not None:
            names = names[2 * half : 2 * half + 2]
        pieces = [env.pop(n) if crossed or n[0] == "k" else env[n] for n in names]
        first = s < 2 and not half
        env["out"] = add_block(
            env.get("out"), shape, place, env[f"scaled{s // 2}"], pieces, half or 0, first, 2 if half is None else 4
        )

    env["coef"], env["slab"] = coef, half_slab
    parts = {f"slab{i}": env["slab"][cuts[i] : cuts[i + 1]] for i in range(1, SLAB_PARTS)}
    step(**line(1), **cross(0), **slab_part(0), **parts, slab_k=over_k(env["slab"]))
    step(**line(2), **cross(1), **slab_part(1), **slab_part_k(0), **cross_k(0))
    step(**line(3), **cross(2), **slab_part(2), **slab_part_k(1), **cross_k(1))
    env["slot3"] = slot(3)
    halves = [env["slot3"][:, c * both : (c + 1) * both] for c in range(PARTS)]
    env.update(later=halves[1])
    step(cross3_0=over_y(halves[0]), kslot3=over_k(env["slot3"]), **slab_part_k(2), **cross_k(2))
    env["kcross3_0"] = over_k(env["cross3_0"])
    step(**transformed(0))

    first = inward(0) | exchange(0) | own_x(0) | cross_core("own0")
    env["cross3_1"] = over_y(env.pop("later"))
    env["kcross3_1"] = over_k(env["cross3_1"])
    step(**first, **transformed(1))
    step(**inward(1), **outward(0), **own_x(1), **cross_core("own1", "own_x0"))
    r = choose(0) | cross_y("o0") | cross_core("o0", "own_x1")
    env.update({n: r.pop(n) for n in ("kown_x1",)})
    step(**r, **exchange(1), **panel(0), **panel(1))
    join(0)
    r = cross_y("c0") | inward(2) | outward(1) | cross_core("yo0")
    block(0, False, cross_core("c0"))
    step(**r)
    r = choose(1) | cross_y("o1") | inward(3) | outward(2) | cross_core("o1")
    block(0, True, cross_core("yc0"))
    step(**r)
    r = choose(2) | cross_y("c1") | outward(3) | cross_core("o2", "yo1")
    block(1, False, cross_core("c1"))
    step(**r)
    join(2)
    r = cross_y("o2") | cross_y("c2") | choose(3) | cross_core("o3")
    block(1, True, cross_core("yc1"))
    block(2, False, cross_core("c2"))
    step(**r)
    r = cross_y("o3") | cross_y("c3")
    block(3, False, cross_core("c3"))
    block(2, True, cross_core("yo2", "yc2"))
    step(**r)
    block(3, True, cross_core("yo3", "yc3"))
    return env["out"]


def solution(mesh):
    in_specs = (P(("row", "col"), None), P("row", "col"), P(), P(), P())
    out_specs = P(None, "row", "col")
    lines = mesh.shape["row"] == 16 and mesh.shape["col"] == 2
    body = line_plan if lines else gathered
    return jax.shard_map(body, mesh=mesh, in_specs=in_specs, out_specs=out_specs, check_vma=False)
```
